32 devices in a mesh: groups: 2 (over x), seg: 16 (over z, y, core).
Axes of the slice: x: 2, y: 2, z: 4, core: 2. Of those that a mesh axis runs over, the one named last changes fastest.
Arguments:
- edge_env: float32 [32, 14, 4, 128, 128], P(('groups', 'seg')), parts along dimension 0, may hold values from -0.5 to 0.5
- start_vector: float32 [32, 2, 128, 512], P(('groups', 'seg')), parts along dimension 0, may hold values from -6 to 6
- mpo: float32 [112, 56], P('groups'), parts along dimension 0, may hold values from -0.75 to 0.75
- sector_map: int32 [14, 4], replicated, may hold values from 0 to 3
Outputs:
- new_vector: float32 [32, 2, 128, 512], P(('groups', 'seg')), parts along dimension 0
- grown_env: float32 [32, 14, 2, 128, 128], P(('groups', 'seg')), parts along dimension 0
- energy: float32 [32], P(('groups', 'seg')), parts along dimension 0
The draws below stay inside these ranges and needn't reach their ends.
There are 2 independent parts, one for each index of `groups`. The reference program is written for one: setup_inputs(seed, part) draws one part's arguments, and reference() takes and returns one part's arrays. A program takes and returns all parts, laid end to end along the dimension named above; an argument that names none is the same for every part. Nothing has to cross between parts.
All inputs are finite; a program needn't handle non-finite values.
Results may differ from the reference program's by a relative error of at most 0.000082.
Values sent between devices are 32-bit elements; how exact they have to be, the bound alone decides.
A program may use at most 128 MiB of HBM per device.

```python
import jax
import jax.numpy as jnp
from jax import lax

B = 128
SECTORS = 4
W = 14
PHYS = 4
N_SEG = 16


def with_ends(values, key, low, top_value):
    dims = values.shape
    place = [jax.random.randint(jax.random.fold_in(key, axis), (), 0, dims[axis]) for axis in range(len(dims))]
    values = values.at[tuple(place)].set(low)
    longest = dims.index(max(dims))
    place[longest] = (place[longest] + 1) % dims[longest]
    return values.at[tuple(place)].set(top_value)


def block_levels(stream_key, extent, split, low, top_value):
    gain, own = 1.0, jax.random.fold_in(stream_key, 6)
    for position, shards_of in split:
        draws = jnp.exp(jax.random.uniform(jax.random.fold_in(own, position), (shards_of,), jnp.float32, low / len(split), top_value / len(split)))
        gain = gain * jnp.repeat(draws, extent[position] // shards_of).reshape([-1 if axis == position else 1 for axis in range(len(extent))])
    return gain


def scatter_about(own_key, shape, width, limit, split=(), dtype=jnp.bfloat16):
    drawn = jax.random.normal(own_key, shape, jnp.float32) * width
    if len(split) > 0:
        drawn = block_levels(own_key, shape, split, -0.22, 0.18) * drawn
    return jnp.clip(drawn, min=-limit, max=limit).astype(dtype)


def setup_inputs(seed: int = 0, part: int = 0) -> dict:
    splits = jax.random.split(jax.random.key(seed), 5)
    part_splits = jax.random.split(jax.random.fold_in(splits[4], part), 5)
    edge_env = scatter_about(part_splits[0], (N_SEG, W, SECTORS, B, B), B ** -0.5, 0.5, ((0, 16),), jnp.float32)
    start_vector = scatter_about(part_splits[1], (N_SEG, SECTORS // 2, B, PHYS * B), 1.0, 6.0, ((0, 16),), jnp.float32)
    mpo = scatter_about(part_splits[2], (W * PHYS, W * PHYS), (W * PHYS) ** -0.5, 0.75, (), jnp.float32)
    sector_map = with_ends(jax.random.randint(splits[3], (W, SECTORS), 0, SECTORS), jax.random.fold_in(splits[3], 1), 0, SECTORS - 1).astype(jnp.int32)
    return dict(edge_env=edge_env, start_vector=start_vector, mpo=mpo, sector_map=sector_map)


precise = lax.Precision.HIGHEST
epsilon = 1e-06

def contract(vector, left_env, src_map, mpo_four):
    gathered = vector[src_map]
    partial_value = jnp.einsum('wtab,wtbx->wtax', left_env, gathered, precision=precise)
    reshaped = partial_value.reshape(partial_value.shape[0], partial_value.shape[1], B, PHYS, B)
    return jnp.einsum('wpvq,wtapb->vtaqb', mpo_four, reshaped, precision=precise)

def apply_env(vector, left_env, right_env, src_map, mpo_four):
    mixed_env = contract(vector, left_env, src_map, mpo_four)
    result = jnp.einsum('vtaqb,vtcb->taqc', mixed_env, right_env, precision=precise)
    return result.reshape(result.shape[0], B, PHYS * B)

def grow_env(fresh_half, fresh_whole, left_env, src_map, mpo_four):
    mixed_env = contract(fresh_whole, left_env, src_map, mpo_four)
    shaped = fresh_half.reshape(fresh_half.shape[0], B, PHYS, B)
    grown = jnp.einsum('taqb,vtaqc->vtbc', shaped, mixed_env, precision=precise)
    return grown / jnp.sqrt(jnp.float32(PHYS * B))

def lowest_pair(ritz_one, ritz_two, coupling):
    half_gap = 0.5 * (ritz_one - ritz_two)
    root_term = jnp.sqrt(half_gap * half_gap + coupling * coupling)
    lowest = 0.5 * (ritz_one + ritz_two) - root_term
    first_coef = root_term - half_gap
    second_coef = -coupling
    length = jnp.sqrt(first_coef * first_coef + second_coef * second_coef)
    return (lowest, first_coef / length, second_coef / length)

def reference(edge_env, start_vector, mpo, sector_map):
    pairs = edge_env.shape[0] // 2
    entries = float(SECTORS * B * PHYS * B)
    envs = edge_env.reshape(2, pairs, W, SECTORS, B, B).transpose(1, 0, 2, 3, 4, 5)
    vectors = start_vector.reshape(2, pairs, SECTORS // 2, B, PHYS * B).transpose(1, 0, 2, 3, 4)
    vectors = vectors.reshape(pairs, SECTORS, B, PHYS * B)
    mpo_four = mpo.reshape(W, PHYS, W, PHYS)

    def solve_pair(pair_item):
        pair_envs, vector = pair_item
        left_env = pair_envs[0]
        right_env = pair_envs[1]
        basis_one = vector / jnp.sqrt(jnp.sum(vector * vector) / entries + epsilon)
        image_one = apply_env(basis_one, left_env, right_env, sector_map, mpo_four)
        ritz_one = jnp.sum(basis_one * image_one) / entries
        residual = image_one - ritz_one * basis_one
        res_norm = jnp.sqrt(jnp.sum(residual * residual) / entries + epsilon)
        basis_two = residual / res_norm
        image_two = apply_env(basis_two, left_env, right_env, sector_map, mpo_four)
        ritz_two = jnp.sum(basis_two * image_two) / entries
        lowest, first_coef, second_coef = lowest_pair(ritz_one, ritz_two, res_norm)
        fresh = first_coef * basis_one + second_coef * basis_two
        grown = grow_env(fresh, fresh, left_env, sector_map, mpo_four)
        return (fresh, grown, lowest)
    fresh, grown, lowest = lax.map(solve_pair, (envs, vectors))
    new_vector = fresh.reshape(pairs, 2, SECTORS // 2, B, PHYS * B).transpose(1, 0, 2, 3, 4)
    new_vector = new_vector.reshape(pairs * 2, SECTORS // 2, B, PHYS * B)
    grown = grown.reshape(pairs, W, 2, SECTORS // 2, B, B).transpose(2, 0, 1, 3, 4, 5)
    grown_env = grown.reshape(pairs * 2, W, SECTORS // 2, B, B)
    energy = jnp.concatenate([lowest, lowest], 0)
    return (new_vector, grown_env, energy)
```

```python
import jax
import jax.numpy as jnp
from jax import lax
from jax.experimental import pallas as pl
from jax.experimental.pallas import tpu as pltpu
from jax.sharding import PartitionSpec as P

epsilon = 1e-06
f32 = jnp.float32
bf16 = jnp.bfloat16


def split(value):
    high = value.astype(bf16)
    low = (value - high.astype(f32)).astype(bf16)
    return high, low


def dot(left, right):
    return lax.dot_general(left, right, (((1,), (0,)), ((), ())), preferred_element_type=f32)


def dot_t(left, right):
    return lax.dot_general(left, right, (((1,), (1,)), ((), ())), preferred_element_type=f32)


def total(value):
    return jnp.sum(jnp.sum(value, axis=0, keepdims=True), axis=1, keepdims=True)


def make_kernel(seg_count, w_dim, sectors, bond, phys):
    halves = sectors // 2
    rows = w_dim * phys
    krows = rows * 8
    entries = float(sectors * bond * phys * bond)

    def kernel(env, start, mpo, smap, fresh_out, grown_out, energy_out,
               lr, v1, w1, vh, vl, xs, yh1, yl1, yh2, yl2, mix3, vt, acc, g11, gx, g22,
               mine, theirs, send, recv, local):
        seg = lax.axis_index("seg")
        upper = seg // (seg_count // 2)
        offset = upper * halves
        other = lax.rem(seg + seg_count // 2, seg_count)
        peer = (lax.axis_index("groups"), other)

        barrier = pltpu.get_barrier_semaphore()
        pl.semaphore_signal(barrier, inc=1, device_id=peer, device_id_type=pl.DeviceIdType.MESH)
        pl.semaphore_wait(barrier, 1)

        def remote(src, dst, index):
            return pltpu.make_async_remote_copy(
                src_ref=src, dst_ref=dst, send_sem=send.at[index], recv_sem=recv.at[index],
                device_id=peer, device_id_type=pl.DeviceIdType.MESH)

        vec_copy = remote(start, v1.at[pl.ds(offset, halves)], 0)
        env_copy = [remote(env.at[:, halves - offset + t], lr.at[upper, t], 1 + t) for t in range(halves)]
        own_vec = pltpu.make_async_copy(start, v1.at[pl.ds(offset, halves)], local.at[0])
        own_env = [pltpu.make_async_copy(env.at[:, offset + t], lr.at[upper, t], local.at[1 + t]) for t in range(halves)]
        vec_copy.start()
        env_copy[0].start()
        own_vec.start()
        for copy in own_env:
            copy.start()

        spread = ((lax.broadcasted_iota(jnp.int32, (krows, rows), 0) >> 3)
                  == lax.broadcasted_iota(jnp.int32, (krows, rows), 1)).astype(f32).astype(bf16)
        eye = ((lax.broadcasted_iota(jnp.int32, (krows, krows), 0) & 7)
               == (lax.broadcasted_iota(jnp.int32, (krows, krows), 1) & 7))
        m_high, m_low = split(mpo[...].T)
        e_high = jnp.where(eye, dot_t(dot(spread, m_high).astype(bf16), spread), 0.0).astype(bf16)
        e_low = jnp.where(eye, dot_t(dot(spread, m_low).astype(bf16), spread), 0.0).astype(bf16)
        mix3[:, :] = jnp.concatenate([e_high, e_high, e_low], axis=1)

        own_vec.wait()
        for copy in own_env:
            copy.wait()
        vec_copy.wait()

        def scale_split(ref, divisor):
            for u in range(sectors):
                value = ref[u] / divisor
                ref[u] = value
                high, low = split(value)
                vh[u] = high
                vl[u] = low

        def turn(ref, place):
            for t in range(halves):
                for s in range(phys):
                    block = ref[offset + t, :, s * bond:(s + 1) * bond].T
                    high, low = split(block)
                    at = slice(place * bond, (place + 1) * bond)
                    vt[t, at, s * bond:(s + 1) * bond] = high
                    vt[t, at, (phys + s) * bond:(phys + s + 1) * bond] = high
                    vt[t, at, (2 * phys + s) * bond:(2 * phys + s + 1) * bond] = low

        def contract(t, y_high, y_low):
            def left(w, carry):
                high, low = split(lr[0, t, w])
                m = smap[w, offset + t]
                v_high = vh[m]
                v_low = vl[m]
                out = dot(jnp.concatenate([high, high, low], axis=1),
                          jnp.concatenate([v_high, v_low, v_high], axis=0))
                for s in range(phys):
                    xs[w * phys + s] = out[:, s * bond:(s + 1) * bond]
                return carry

            lax.fori_loop(0, w_dim, left, 0, unroll=2)

            def mix(j, carry):
                first = xs[:, pl.ds(j * 16, 8), :].reshape(krows, bond)
                second = xs[:, pl.ds(j * 16 + 8, 8), :].reshape(krows, bond)
                high, low = split(jnp.concatenate([first, second], axis=1))
                out = dot(mix3[...], jnp.concatenate([high, low, high], axis=0))
                both = jnp.concatenate([out[:, :bond].reshape(rows, 8, bond),
                                        out[:, bond:].reshape(rows, 8, bond)], axis=1)
                high, low = split(both)
                y_high[t, :, pl.ds(j * 16, 16), :] = high
                y_low[t, :, pl.ds(j * 16, 16), :] = low
                return carry

            lax.fori_loop(0, bond // 16, mix, 0)

        def right(t):
            acc[...] = jnp.zeros_like(acc)

            def step(w, carry):
                r_high, r_low = split(lr[1, t, w])
                high = yh1[t, pl.ds(w * phys, phys)].reshape(phys * bond, bond)
                low = yl1[t, pl.ds(w * phys, phys)].reshape(phys * bond, bond)
                acc[...] += dot_t(jnp.concatenate([high, high, low], axis=1),
                                  jnp.concatenate([r_high, r_low, r_high], axis=1))
                return carry

            lax.fori_loop(0, w_dim, step, 0, unroll=2)
            for s in range(phys):
                w1[offset + t, :, s * bond:(s + 1) * bond] = acc[s * bond:(s + 1) * bond, :]

        def stacked(y_high, y_low, t, w):
            high = y_high[t, pl.ds(w * phys, phys)].reshape(phys * bond, bond)
            low = y_low[t, pl.ds(w * phys, phys)].reshape(phys * bond, bond)
            return jnp.concatenate([high, low, high], axis=0)

        norm = epsilon + sum(total(v1[u] * v1[u]) for u in range(sectors)) / entries
        scale_split(v1, jnp.sqrt(norm))
        turn(v1, 0)

        env_copy[0].wait_send()
        for copy in env_copy[1:]:
            copy.start()
        w_copy = [remote(w1.at[offset + t], w1.at[offset + t], 1 + halves + t) for t in range(halves)]
        for t in range(halves):
            env_copy[t].wait_recv()
            contract(t, yh1, yl1)
            right(t)
            w_copy[t].start()
        for copy in env_copy[1:]:
            copy.wait_send()

        def grow_one(w, carry):
            for t in range(halves):
                g11[w, t] = dot(vt[t, :bond, :], stacked(yh1, yl1, t, w))
            return carry

        lax.fori_loop(0, w_dim, grow_one, 0)
        for copy in w_copy:
            copy.wait()

        r1 = sum(total(v1[u] * w1[u]) for u in range(sectors)) / entries
        square = 0.0
        for u in range(sectors):
            res = w1[u] - r1 * v1[u]
            w1[u] = res
            square = square + total(res * res)
        q = jnp.sqrt(square / entries + epsilon)
        scale_split(w1, q)
        for t in range(halves):
            contract(t, yh2, yl2)
        turn(w1, 1)

        mine[...] = jnp.zeros_like(mine)

        def grow_two(w, carry):
            for t in range(halves):
                out = dot(vt[t], stacked(yh2, yl2, t, w))
                gx[w, t] = out[:bond]
                g22[w, t] = out[bond:]
                prod = out[bond:] * lr[1, t, w]
                mine[...] += jnp.sum(prod.reshape(bond // 8, 8, bond), axis=0)
            return carry

        lax.fori_loop(0, w_dim, grow_two, 0)
        r_copy = remote(mine, theirs, 1 + 2 * halves)
        r_copy.start()

        def grow_three(w, carry):
            for t in range(halves):
                gx[w, t] += dot(vt[t, bond:, :], stacked(yh1, yl1, t, w))
            return carry

        lax.fori_loop(0, w_dim, grow_three, 0)
        r_copy.wait()
        r2 = total(mine[...] + theirs[...]) / entries
        g = 0.5 * (r1 - r2)
        root = jnp.sqrt(g * g + q * q)
        energy_out[...] = jnp.broadcast_to(0.5 * (r1 + r2) - root, energy_out.shape)
        x = root - g
        y = -q
        length = jnp.sqrt(x * x + y * y)
        x = x / length
        y = y / length
        for t in range(halves):
            fresh_out[t] = x * v1[offset + t] + y * w1[offset + t]
        scale = 1.0 / jnp.sqrt(f32(phys * bond))
        c11 = x * x * scale
        c12 = x * y * scale
        c22 = y * y * scale

        def finish(w, carry):
            for t in range(halves):
                grown_out[w, t] = c11 * g11[w, t] + c12 * gx[w, t] + c22 * g22[w, t]
            return carry

        lax.fori_loop(0, w_dim, finish, 0)

    return kernel


def shards(edge_env, start_vector, mpo, sector_map):
    _, w_dim, sectors, bond, _ = edge_env.shape
    phys = start_vector.shape[3] // bond
    halves = sectors // 2
    rows = w_dim * phys
    krows = rows * 8
    seg_count = lax.axis_size("seg")
    vmem = pl.BlockSpec(memory_space=pltpu.VMEM)
    hbm = pl.BlockSpec(memory_space=pl.ANY)
    smem = pl.BlockSpec(memory_space=pltpu.SMEM)
    wide = (sectors, bond, phys * bond)
    big = (halves, rows, bond, bond)
    env = (w_dim, halves, bond, bond)
    fresh, grown, energy = pl.pallas_call(
        make_kernel(seg_count, w_dim, sectors, bond, phys),
        out_shape=(
            jax.ShapeDtypeStruct((halves, bond, phys * bond), f32),
            jax.ShapeDtypeStruct(env, f32),
            jax.ShapeDtypeStruct((8, 128), f32),
        ),
        in_specs=[hbm, hbm, vmem, smem],
        out_specs=(vmem, vmem, vmem),
        scratch_shapes=[
            pltpu.VMEM((2, halves, w_dim, bond, bond), f32),
            pltpu.VMEM(wide, f32),
            pltpu.VMEM(wide, f32),
            pltpu.VMEM(wide, bf16),
            pltpu.VMEM(wide, bf16),
            pltpu.VMEM((rows, bond, bond), f32),
            pltpu.VMEM(big, bf16),
            pltpu.VMEM(big, bf16),
            pltpu.VMEM(big, bf16),
            pltpu.VMEM(big, bf16),
            pltpu.VMEM((krows, 3 * krows), bf16),
            pltpu.VMEM((halves, 2 * bond, 3 * phys * bond), bf16),
            pltpu.VMEM((phys * bond, bond), f32),
            pltpu.VMEM(env, f32),
            pltpu.VMEM(env, f32),
            pltpu.VMEM(env, f32),
            pltpu.VMEM((8, 128), f32),
            pltpu.VMEM((8, 128), f32),
            pltpu.SemaphoreType.DMA((2 + 2 * halves,)),
            pltpu.SemaphoreType.DMA((2 + 2 * halves,)),
            pltpu.SemaphoreType.DMA((1 + halves,)),
        ],
        compiler_params=pltpu.CompilerParams(
            collective_id=0, has_side_effects=True, vmem_limit_bytes=56 * 1024 * 1024),
    )(edge_env[0], start_vector[0], mpo, sector_map)
    return (fresh[None], grown[None], energy[0, :1])


def solution(mesh):
    placed = (
        P(("groups", "seg"), None, None, None, None),
        P(("groups", "seg"), None, None, None),
        P("groups", None),
        P(),
    )
    return jax.shard_map(
        shards,
        mesh=mesh,
        in_specs=placed,
        out_specs=(
            P(("groups", "seg"), None, None, None),
            P(("groups", "seg"), None, None, None, None),
            P(("groups", "seg")),
        ),
        check_vma=False,
    )
```

```python
import jax
import jax.numpy as jnp
from jax import lax
from jax.experimental import pallas as pl
from jax.experimental.pallas import tpu as pltpu
from jax.sharding import PartitionSpec as P

epsilon = 1e-06
f32 = jnp.float32
bf16 = jnp.bfloat16


def split(value):
    high = value.astype(bf16)
    low = (value - high.astype(f32)).astype(bf16)
    return high, low


def dot(left, right):
    return lax.dot_general(left, right, (((1,), (0,)), ((), ())), preferred_element_type=f32)


def dot_t(left, right):
    return lax.dot_general(left, right, (((1,), (1,)), ((), ())), preferred_element_type=f32)


def total(value):
    return jnp.sum(jnp.sum(value, axis=0, keepdims=True), axis=1, keepdims=True)


def make_kernel(seg_count, w_dim, sectors, bond, phys):
    halves = sectors // 2
    rows = w_dim * phys
    krows = rows * 8
    entries = float(sectors * bond * phys * bond)

    def kernel(env, start, mpo, smap, fresh_out, grown_out, energy_out,
               lr, v1, w1, vh, vl, xs, yh1, yl1, yh2, yl2, mix3, vt, acc, g11, gx, g22,
               mine, theirs, send, recv, local):
        seg = lax.axis_index("seg")
        upper = seg // (seg_count // 2)
        offset = upper * halves
        other = lax.rem(seg + seg_count // 2, seg_count)
        peer = (lax.axis_index("groups"), other)

        barrier = pltpu.get_barrier_semaphore()
        pl.semaphore_signal(barrier, inc=1, device_id=peer, device_id_type=pl.DeviceIdType.MESH)
        pl.semaphore_wait(barrier, 1)

        def remote(src, dst, index):
            return pltpu.make_async_remote_copy(
                src_ref=src, dst_ref=dst, send_sem=send.at[index], recv_sem=recv.at[index],
                device_id=peer, device_id_type=pl.DeviceIdType.MESH)

        vec_copy = remote(start, v1.at[pl.ds(offset, halves)], 0)
        env_copy = [remote(env.at[:, halves - offset + t], lr.at[upper, t], 1 + t) for t in range(halves)]
        own_vec = pltpu.make_async_copy(start, v1.at[pl.ds(offset, halves)], local.at[0])
        own_env = [pltpu.make_async_copy(env.at[:, offset + t], lr.at[upper, t], local.at[1 + t]) for t in range(halves)]
        vec_copy.start()
        env_copy[0].start()
        own_vec.start()
        for copy in own_env:
            copy.start()

        spread = ((lax.broadcasted_iota(jnp.int32, (krows, rows), 0) >> 3)
                  == lax.broadcasted_iota(jnp.int32, (krows, rows), 1)).astype(f32).astype(bf16)
        eye = ((lax.broadcasted_iota(jnp.int32, (krows, krows), 0) & 7)
               == (lax.broadcasted_iota(jnp.int32, (krows, krows), 1) & 7))
        m_high, m_low = split(mpo[...].T)
        e_high = jnp.where(eye, dot_t(dot(spread, m_high).astype(bf16), spread), 0.0).astype(bf16)
        e_low = jnp.where(eye, dot_t(dot(spread, m_low).astype(bf16), spread), 0.0).astype(bf16)
        mix3[:, :] = jnp.concatenate([e_high, e_high, e_low], axis=1)

        own_vec.wait()
        for copy in own_env:
            copy.wait()
        vec_copy.wait()

        def scale_split(ref, divisor):
            for u in range(sectors):
                value = ref[u] / divisor
                ref[u] = value
                high, low = split(value)
                vh[u] = high
                vl[u] = low

        def turn(ref, place):
            for t in range(halves):
                for s in range(phys):
                    block = ref[offset + t, :, s * bond:(s + 1) * bond].T
                    high, low = split(block)
                    at = slice(place * bond, (place + 1) * bond)
                    vt[t, at, s * bond:(s + 1) * bond] = high
                    vt[t, at, (phys + s) * bond:(phys + s + 1) * bond] = high
                    vt[t, at, (2 * phys + s) * bond:(2 * phys + s + 1) * bond] = low

        def contract(t, y_high, y_low):
            def left(w, carry):
                high, low = split(lr[0, t, w])
                m = smap[offset + t, w]
                v_high = vh[m]
                v_low = vl[m]
                out = dot(jnp.concatenate([high, high, low], axis=1),
                          jnp.concatenate([v_high, v_low, v_high], axis=0))
                for s in range(phys):
                    xs[w * phys + s] = out[:, s * bond:(s + 1) * bond]
                return carry

            lax.fori_loop(0, w_dim, left, 0, unroll=7)

            def mix(j, carry):
                first = xs[:, pl.ds(j * 16, 8), :].reshape(krows, bond)
                second = xs[:, pl.ds(j * 16 + 8, 8), :].reshape(krows, bond)
                high, low = split(jnp.concatenate([first, second], axis=1))
                out = dot(mix3[...], jnp.concatenate([high, low, high], axis=0))
                both = jnp.concatenate([out[:, :bond].reshape(rows, 8, bond),
                                        out[:, bond:].reshape(rows, 8, bond)], axis=1)
                high, low = split(both)
                y_high[t, :, pl.ds(j * 16, 16), :] = high
                y_low[t, :, pl.ds(j * 16, 16), :] = low
                return carry

            lax.fori_loop(0, bond // 16, mix, 0, unroll=4)

        def right(t):
            acc[...] = jnp.zeros_like(acc)

            def step(i, carry):
                ys, rs = [], []
                for j in range(2):
                    w = 2 * i + j
                    r_high, r_low = split(lr[1, t, w])
                    high = yh1[t, pl.ds(w * phys, phys)].reshape(phys * bond, bond)
                    low = yl1[t, pl.ds(w * phys, phys)].reshape(phys * bond, bond)
                    ys += [high, high, low]
                    rs += [r_high, r_low, r_high]
                acc[...] += dot_t(jnp.concatenate(ys, axis=1), jnp.concatenate(rs, axis=1))
                return carry

            lax.fori_loop(0, w_dim // 2, step, 0)
            for s in range(phys):
                w1[offset + t, :, s * bond:(s + 1) * bond] = acc[s * bond:(s + 1) * bond, :]

        def stacked(y_high, y_low, t, i):
            pair = []
            for j in range(2):
                at = pl.ds((2 * i + j) * phys, phys)
                high = y_high[t, at].reshape(phys * bond, bond)
                low = y_low[t, at].reshape(phys * bond, bond)
                pair.append(jnp.concatenate([high, low, high], axis=0))
            return jnp.concatenate(pair, axis=1)

        norm = epsilon + sum(total(v1[u] * v1[u]) for u in range(sectors)) / entries
        scale_split(v1, jnp.sqrt(norm))
        turn(v1, 0)

        env_copy[0].wait_send()
        env_copy[1].start()
        w_copy = [remote(w1.at[offset + t], w1.at[offset + t], 1 + halves + t) for t in range(halves)]
        for t in range(halves):
            env_copy[t].wait_recv()
            contract(t, yh1, yl1)
            right(t)
            if t + 1 < halves:
                env_copy[t + 1].wait_send()
            w_copy[t].start()

        def grow_one(i, carry):
            for t in range(halves):
                out = dot(vt[t, :bond, :], stacked(yh1, yl1, t, i))
                for j in range(2):
                    g11[2 * i + j, t] = out[:, j * bond:(j + 1) * bond]
            return carry

        lax.fori_loop(0, w_dim // 2, grow_one, 0)
        for copy in w_copy:
            copy.wait()

        r1 = sum(total(v1[u] * w1[u]) for u in range(sectors)) / entries
        square = 0.0
        for u in range(sectors):
            res = w1[u] - r1 * v1[u]
            w1[u] = res
            square = square + total(res * res)
        q = jnp.sqrt(square / entries + epsilon)
        scale_split(w1, q)
        for t in range(halves):
            contract(t, yh2, yl2)
        turn(w1, 1)

        mine[...] = jnp.zeros_like(mine)

        def grow_two(i, carry):
            for t in range(halves):
                out = dot(vt[t], stacked(yh2, yl2, t, i))
                for j in range(2):
                    w = 2 * i + j
                    gx[w, t] = out[:bond, j * bond:(j + 1) * bond]
                    part = out[bond:, j * bond:(j + 1) * bond]
                    g22[w, t] = part
                    prod = part * lr[1, t, w]
                    mine[...] += jnp.sum(prod.reshape(bond // 8, 8, bond), axis=0)
            return carry

        lax.fori_loop(0, w_dim // 2, grow_two, 0)
        r_copy = remote(mine, theirs, 1 + 2 * halves)
        r_copy.start()

        def grow_three(i, carry):
            for t in range(halves):
                out = dot(vt[t, bond:, :], stacked(yh1, yl1, t, i))
                for j in range(2):
                    gx[2 * i + j, t] += out[:, j * bond:(j + 1) * bond]
            return carry

        lax.fori_loop(0, w_dim // 2, grow_three, 0)
        r_copy.wait()
        r2 = total(mine[...] + theirs[...]) / entries
        g = 0.5 * (r1 - r2)
        root = jnp.sqrt(g * g + q * q)
        energy_out[...] = jnp.broadcast_to(0.5 * (r1 + r2) - root, energy_out.shape)
        x = root - g
        y = -q
        length = jnp.sqrt(x * x + y * y)
        x = x / length
        y = y / length
        for t in range(halves):
            fresh_out[t] = x * v1[offset + t] + y * w1[offset + t]
        scale = 1.0 / jnp.sqrt(f32(phys * bond))
        c11 = x * x * scale
        c12 = x * y * scale
        c22 = y * y * scale

        def finish(w, carry):
            for t in range(halves):
                grown_out[w, t] = c11 * g11[w, t] + c12 * gx[w, t] + c22 * g22[w, t]
            return carry

        lax.fori_loop(0, w_dim, finish, 0)

    return kernel


def place(fresh, grown, energy, fresh_out, grown_out, energy_out, fresh_buf, grown_buf, sems, out_sems):
    w_dim = grown.shape[0]
    parts = [(grown.at[pl.ds(i, 2)], grown_buf.at[pl.ds(i, 2)], grown_out.at[pl.ds(i, 2)]) for i in range(0, w_dim, 2)]
    parts.append((fresh, fresh_buf, fresh_out))
    ins = [pltpu.make_async_copy(src, buf, sems.at[i]) for i, (src, buf, _) in enumerate(parts)]
    outs = [pltpu.make_async_copy(buf, dst, out_sems.at[i]) for i, (_, buf, dst) in enumerate(parts)]
    for copy in ins:
        copy.start()
    energy_out[...] = energy[...]
    for copy, after in zip(ins, outs):
        copy.wait()
        after.start()
    for copy in outs:
        copy.wait()


def shards(edge_env, start_vector, mpo, sector_map):
    _, w_dim, sectors, bond, _ = edge_env.shape
    phys = start_vector.shape[3] // bond
    halves = sectors // 2
    rows = w_dim * phys
    krows = rows * 8
    seg_count = lax.axis_size("seg")
    vmem = pl.BlockSpec(memory_space=pltpu.VMEM)
    hbm = pl.BlockSpec(memory_space=pl.ANY)
    smem = pl.BlockSpec(memory_space=pltpu.SMEM)
    wide = (sectors, bond, phys * bond)
    big = (halves, rows, bond, bond)
    env = (w_dim, halves, bond, bond)
    fresh, grown, energy = pl.pallas_call(
        make_kernel(seg_count, w_dim, sectors, bond, phys),
        out_shape=(
            jax.ShapeDtypeStruct((halves, bond, phys * bond), f32),
            jax.ShapeDtypeStruct(env, f32),
            jax.ShapeDtypeStruct((1, 1), f32),
        ),
        in_specs=[hbm, hbm, vmem, smem],
        out_specs=(vmem, vmem, vmem),
        scratch_shapes=[
            pltpu.VMEM((2, halves, w_dim, bond, bond), f32),
            pltpu.VMEM(wide, f32),
            pltpu.VMEM(wide, f32),
            pltpu.VMEM(wide, bf16),
            pltpu.VMEM(wide, bf16),
            pltpu.VMEM((rows, bond, bond), f32),
            pltpu.VMEM(big, bf16),
            pltpu.VMEM(big, bf16),
            pltpu.VMEM(big, bf16),
            pltpu.VMEM(big, bf16),
            pltpu.VMEM((krows, 3 * krows), bf16),
            pltpu.VMEM((halves, 2 * bond, 3 * phys * bond), bf16),
            pltpu.VMEM((phys * bond, bond), f32),
            pltpu.VMEM(env, f32),
            pltpu.VMEM(env, f32),
            pltpu.VMEM(env, f32),
            pltpu.VMEM((8, 128), f32),
            pltpu.VMEM((8, 128), f32),
            pltpu.SemaphoreType.DMA((2 + 2 * halves,)),
            pltpu.SemaphoreType.DMA((2 + 2 * halves,)),
            pltpu.SemaphoreType.DMA((1 + halves,)),
        ],
        compiler_params=pltpu.CompilerParams(
            collective_id=0, has_side_effects=True, vmem_limit_bytes=56 * 1024 * 1024),
    )(edge_env[0], start_vector[0], mpo, sector_map.T)
    fresh, grown, energy = pl.pallas_call(
        place,
        out_shape=tuple(jax.ShapeDtypeStruct(value.shape, f32) for value in (fresh, grown, energy)),
        in_specs=[hbm, hbm, vmem],
        out_specs=(hbm, hbm, vmem),
        scratch_shapes=[
            pltpu.VMEM(fresh.shape, f32),
            pltpu.VMEM(grown.shape, f32),
            pltpu.SemaphoreType.DMA((w_dim // 2 + 1,)),
            pltpu.SemaphoreType.DMA((w_dim // 2 + 1,)),
        ],
    )(fresh, grown, energy)
    return (fresh[None], grown[None], energy.reshape(1))


def solution(mesh):
    placed = (
        P(("groups", "seg"), None, None, None, None),
        P(("groups", "seg"), None, None, None),
        P("groups", None),
        P(),
    )
    return jax.shard_map(
        shards,
        mesh=mesh,
        in_specs=placed,
        out_specs=(
            P(("groups", "seg"), None, None, None),
            P(("groups", "seg"), None, None, None, None),
            P(("groups", "seg")),
        ),
        check_vma=False,
    )
```

```python
import jax
import jax.numpy as jnp
from jax import lax
from jax.experimental import pallas as pl
from jax.experimental.pallas import tpu as pltpu
from jax.sharding import PartitionSpec as P

epsilon = 1e-06
f32 = jnp.float32
bf16 = jnp.bfloat16


def split(value):
    high = value.astype(bf16)
    low = (value - high.astype(f32)).astype(bf16)
    return high, low


def dot(left, right):
    return lax.dot_general(left, right, (((1,), (0,)), ((), ())), preferred_element_type=f32)


def dot_t(left, right):
    return lax.dot_general(left, right, (((1,), (1,)), ((), ())), preferred_element_type=f32)


def total(value):
    return jnp.sum(jnp.sum(value, axis=0, keepdims=True), axis=1, keepdims=True)


def make_kernel(seg_count, w_dim, sectors, bond, phys):
    halves = sectors // 2
    rows = w_dim * phys
    krows = rows * 8
    entries = float(sectors * bond * phys * bond)

    def kernel(env, start, mpo, smap, fresh_out, grown_out, energy_out,
               lr, v1, w1, vh, vl, xs, yh1, yl1, yh2, yl2, mix3, vt, acc, g11, gx, g22,
               mine, theirs, send, recv, local):
        seg = lax.axis_index("seg")
        upper = seg // (seg_count // 2)
        offset = upper * halves
        other = lax.rem(seg + seg_count // 2, seg_count)
        peer = (lax.axis_index("groups"), other)

        barrier = pltpu.get_barrier_semaphore()
        pl.semaphore_signal(barrier, inc=1, device_id=peer, device_id_type=pl.DeviceIdType.MESH)
        pl.semaphore_wait(barrier, 1)

        def remote(src, dst, index):
            return pltpu.make_async_remote_copy(
                src_ref=src, dst_ref=dst, send_sem=send.at[index], recv_sem=recv.at[index],
                device_id=peer, device_id_type=pl.DeviceIdType.MESH)

        vec_copy = remote(start, v1.at[pl.ds(offset, halves)], 0)
        env_copy = [remote(env.at[cut, halves - offset + t], lr.at[upper, t, cut], i)
                    for i, t, cut in ((1, 0, pl.ds(0, w_dim // 2)), (2, 0, pl.ds(w_dim // 2, w_dim // 2)),
                                      (3, 1, pl.ds(0, w_dim)))]
        own_vec = pltpu.make_async_copy(start, v1.at[pl.ds(offset, halves)], local.at[0])
        own_env = [pltpu.make_async_copy(env.at[:, offset + t], lr.at[upper, t], local.at[1 + t]) for t in range(halves)]
        vec_copy.start()
        env_copy[0].start()
        own_vec.start()
        for copy in own_env:
            copy.start()

        spread = ((lax.broadcasted_iota(jnp.int32, (krows, rows), 0) >> 3)
                  == lax.broadcasted_iota(jnp.int32, (krows, rows), 1)).astype(f32).astype(bf16)
        eye = ((lax.broadcasted_iota(jnp.int32, (krows, krows), 0) & 7)
               == (lax.broadcasted_iota(jnp.int32, (krows, krows), 1) & 7))
        m_high, m_low = split(mpo[...].T)
        e_high = jnp.where(eye, dot_t(dot(spread, m_high).astype(bf16), spread), 0.0).astype(bf16)
        e_low = jnp.where(eye, dot_t(dot(spread, m_low).astype(bf16), spread), 0.0).astype(bf16)
        mix3[:, :] = jnp.concatenate([e_high, e_high, e_low], axis=1)

        own_vec.wait()
        for copy in own_env:
            copy.wait()
        vec_copy.wait()
        env_copy[1].start()

        def scale_split(ref, divisor):
            for u in range(sectors):
                value = ref[u] / divisor
                ref[u] = value
                high, low = split(value)
                vh[u] = high
                vl[u] = low

        def turn(ref, place):
            for t in range(halves):
                for s in range(phys):
                    block = ref[offset + t, :, s * bond:(s + 1) * bond].T
                    high, low = split(block)
                    at = slice(place * bond, (place + 1) * bond)
                    vt[t, at, s * bond:(s + 1) * bond] = high
                    vt[t, at, (phys + s) * bond:(phys + s + 1) * bond] = high
                    vt[t, at, (2 * phys + s) * bond:(2 * phys + s + 1) * bond] = low

        def contract(t, y_high, y_low):
            def left(w, carry):
                high, low = split(lr[0, t, w])
                m = smap[offset + t, w]
                v_high = vh[m]
                v_low = vl[m]
                out = dot(jnp.concatenate([high, high, low], axis=1),
                          jnp.concatenate([v_high, v_low, v_high], axis=0))
                for s in range(phys):
                    xs[w * phys + s] = out[:, s * bond:(s + 1) * bond]
                return carry

            lax.fori_loop(0, w_dim, left, 0, unroll=7)

            def mix(j, carry):
                first = xs[:, pl.ds(j * 16, 8), :].reshape(krows, bond)
                second = xs[:, pl.ds(j * 16 + 8, 8), :].reshape(krows, bond)
                high, low = split(jnp.concatenate([first, second], axis=1))
                out = dot(mix3[...], jnp.concatenate([high, low, high], axis=0))
                both = jnp.concatenate([out[:, :bond].reshape(rows, 8, bond),
                                        out[:, bond:].reshape(rows, 8, bond)], axis=1)
                high, low = split(both)
                y_high[t, :, pl.ds(j * 16, 16), :] = high
                y_low[t, :, pl.ds(j * 16, 16), :] = low
                return carry

            lax.fori_loop(0, bond // 16, mix, 0, unroll=4)

        def right(t):
            acc[...] = jnp.zeros_like(acc)

            def step(i, carry):
                ys, rs = [], []
                for j in range(2):
                    w = 2 * i + j
                    r_high, r_low = split(lr[1, t, w])
                    high = yh1[t, pl.ds(w * phys, phys)].reshape(phys * bond, bond)
                    low = yl1[t, pl.ds(w * phys, phys)].reshape(phys * bond, bond)
                    ys += [high, high, low]
                    rs += [r_high, r_low, r_high]
                acc[...] += dot_t(jnp.concatenate(ys, axis=1), jnp.concatenate(rs, axis=1))
                return carry

            lax.fori_loop(0, w_dim // 2, step, 0)
            for s in range(phys):
                w1[offset + t, :, s * bond:(s + 1) * bond] = acc[s * bond:(s + 1) * bond, :]

        def stacked(y_high, y_low, t, i):
            pair = []
            for j in range(2):
                at = pl.ds((2 * i + j) * phys, phys)
                high = y_high[t, at].reshape(phys * bond, bond)
                low = y_low[t, at].reshape(phys * bond, bond)
                pair.append(jnp.concatenate([high, low, high], axis=0))
            return jnp.concatenate(pair, axis=1)

        norm = epsilon + sum(total(v1[u] * v1[u]) for u in range(sectors)) / entries
        scale_split(v1, jnp.sqrt(norm))
        turn(v1, 0)

        env_copy[0].wait_send()
        env_copy[2].start()
        env_copy[1].wait_send()
        w_copy = [remote(w1.at[offset + t], w1.at[offset + t], 2 + halves + t) for t in range(halves)]
        for t in range(halves):
            for copy in (env_copy[:2], env_copy[2:])[t]:
                copy.wait_recv()
            contract(t, yh1, yl1)
            right(t)
            if t + 1 < halves:
                env_copy[2].wait_send()
            w_copy[t].start()

        def grow_one(i, carry):
            for t in range(halves):
                out = dot(vt[t, :bond, :], stacked(yh1, yl1, t, i))
                for j in range(2):
                    g11[2 * i + j, t] = out[:, j * bond:(j + 1) * bond]
            return carry

        lax.fori_loop(0, w_dim // 2, grow_one, 0)
        for copy in w_copy:
            copy.wait()

        r1 = sum(total(v1[u] * w1[u]) for u in range(sectors)) / entries
        square = 0.0
        for u in range(sectors):
            res = w1[u] - r1 * v1[u]
            w1[u] = res
            square = square + total(res * res)
        q = jnp.sqrt(square / entries + epsilon)
        scale_split(w1, q)
        for t in range(halves):
            contract(t, yh2, yl2)
        turn(w1, 1)

        mine[...] = jnp.zeros_like(mine)

        def grow_two(i, carry):
            for t in range(halves):
                out = dot(vt[t], stacked(yh2, yl2, t, i))
                for j in range(2):
                    w = 2 * i + j
                    gx[w, t] = out[:bond, j * bond:(j + 1) * bond]
                    part = out[bond:, j * bond:(j + 1) * bond]
                    g22[w, t] = part
                    prod = part * lr[1, t, w]
                    mine[...] += jnp.sum(prod.reshape(bond // 8, 8, bond), axis=0)
            return carry

        lax.fori_loop(0, w_dim // 2, grow_two, 0, unroll=7)
        r_copy = remote(mine, theirs, 2 + 2 * halves)
        r_copy.start()

        def grow_three(i, carry):
            for t in range(halves):
                out = dot(vt[t, bond:, :], stacked(yh1, yl1, t, i))
                for j in range(2):
                    gx[2 * i + j, t] += out[:, j * bond:(j + 1) * bond]
            return carry

        lax.fori_loop(0, w_dim // 2, grow_three, 0)
        r_copy.wait()
        r2 = total(mine[...] + theirs[...]) / entries
        g = 0.5 * (r1 - r2)
        root = jnp.sqrt(g * g + q * q)
        energy_out[...] = jnp.broadcast_to(0.5 * (r1 + r2) - root, energy_out.shape)
        x = root - g
        y = -q
        length = jnp.sqrt(x * x + y * y)
        x = x / length
        y = y / length
        for t in range(halves):
            fresh_out[t] = x * v1[offset + t] + y * w1[offset + t]
        scale = 1.0 / jnp.sqrt(f32(phys * bond))
        c11 = x * x * scale
        c12 = x * y * scale
        c22 = y * y * scale

        def finish(w, carry):
            for t in range(halves):
                grown_out[w, t] = c11 * g11[w, t] + c12 * gx[w, t] + c22 * g22[w, t]
            return carry

        lax.fori_loop(0, w_dim, finish, 0, unroll=7)

    return kernel


def place(fresh, grown, energy, fresh_out, grown_out, energy_out, fresh_buf, grown_buf, sems, out_sems):
    w_dim = grown.shape[0]
    parts = [(grown.at[pl.ds(i, 2)], grown_buf.at[pl.ds(i, 2)], grown_out.at[pl.ds(i, 2)]) for i in range(0, w_dim, 2)]
    parts.append((fresh, fresh_buf, fresh_out))
    ins = [pltpu.make_async_copy(src, buf, sems.at[i]) for i, (src, buf, _) in enumerate(parts)]
    outs = [pltpu.make_async_copy(buf, dst, out_sems.at[i]) for i, (_, buf, dst) in enumerate(parts)]
    for copy in ins:
        copy.start()
    energy_out[...] = energy[...]
    for copy, after in zip(ins, outs):
        copy.wait()
        after.start()
    for copy in outs:
        copy.wait()


def shards(edge_env, start_vector, mpo, sector_map):
    _, w_dim, sectors, bond, _ = edge_env.shape
    phys = start_vector.shape[3] // bond
    halves = sectors // 2
    rows = w_dim * phys
    krows = rows * 8
    seg_count = lax.axis_size("seg")
    vmem = pl.BlockSpec(memory_space=pltpu.VMEM)
    hbm = pl.BlockSpec(memory_space=pl.ANY)
    smem = pl.BlockSpec(memory_space=pltpu.SMEM)
    wide = (sectors, bond, phys * bond)
    big = (halves, rows, bond, bond)
    env = (w_dim, halves, bond, bond)
    fresh, grown, energy = pl.pallas_call(
        make_kernel(seg_count, w_dim, sectors, bond, phys),
        out_shape=(
            jax.ShapeDtypeStruct((halves, bond, phys * bond), f32),
            jax.ShapeDtypeStruct(env, f32),
            jax.ShapeDtypeStruct((1, 1), f32),
        ),
        in_specs=[hbm, hbm, vmem, smem],
        out_specs=(vmem, vmem, vmem),
        scratch_shapes=[
            pltpu.VMEM((2, halves, w_dim, bond, bond), f32),
            pltpu.VMEM(wide, f32),
            pltpu.VMEM(wide, f32),
            pltpu.VMEM(wide, bf16),
            pltpu.VMEM(wide, bf16),
            pltpu.VMEM((rows, bond, bond), f32),
            pltpu.VMEM(big, bf16),
            pltpu.VMEM(big, bf16),
            pltpu.VMEM(big, bf16),
            pltpu.VMEM(big, bf16),
            pltpu.VMEM((krows, 3 * krows), bf16),
            pltpu.VMEM((halves, 2 * bond, 3 * phys * bond), bf16),
            pltpu.VMEM((phys * bond, bond), f32),
            pltpu.VMEM(env, f32),
            pltpu.VMEM(env, f32),
            pltpu.VMEM(env, f32),
            pltpu.VMEM((8, 128), f32),
            pltpu.VMEM((8, 128), f32),
            pltpu.SemaphoreType.DMA((3 + 2 * halves,)),
            pltpu.SemaphoreType.DMA((3 + 2 * halves,)),
            pltpu.SemaphoreType.DMA((1 + halves,)),
        ],
        compiler_params=pltpu.CompilerParams(
            collective_id=0, has_side_effects=True, vmem_limit_bytes=56 * 1024 * 1024),
    )(edge_env[0], start_vector[0], mpo, sector_map.T)
    fresh, grown, energy = pl.pallas_call(
        place,
        out_shape=tuple(jax.ShapeDtypeStruct(value.shape, f32) for value in (fresh, grown, energy)),
        in_specs=[hbm, hbm, vmem],
        out_specs=(hbm, hbm, vmem),
        scratch_shapes=[
            pltpu.VMEM(fresh.shape, f32),
            pltpu.VMEM(grown.shape, f32),
            pltpu.SemaphoreType.DMA((w_dim // 2 + 1,)),
            pltpu.SemaphoreType.DMA((w_dim // 2 + 1,)),
        ],
    )(fresh, grown, energy)
    return (fresh[None], grown[None], energy.reshape(1))


def solution(mesh):
    placed = (
        P(("groups", "seg"), None, None, None, None),
        P(("groups", "seg"), None, None, None),
        P("groups", None),
        P(),
    )
    return jax.shard_map(
        shards,
        mesh=mesh,
        in_specs=placed,
        out_specs=(
            P(("groups", "seg"), None, None, None),
            P(("groups", "seg"), None, None, None, None),
            P(("groups", "seg")),
        ),
        check_vma=False,
    )
```
